512 devices in a mesh: row: 64 (over z, x, y_hi), col: 8 (over y_lo, core).
Axes of the slice: x: 4, y: 8 (y_hi: 2, y_lo: 4; y = y_hi * 4 + y_lo), z: 8, core: 2. Of those that a mesh axis runs over, the one named last changes fastest.
Arguments:
- inputs: bfloat16 [256, 12288], P('row', 'col'), may hold values from -6 to 6
- up_weight: bfloat16 [12288, 24576], P('col', 'row'), may hold values from -0.109375 to 0.109375
- down_weight: bfloat16 [24576, 12288], P('row', 'col'), may hold values from -0.078125 to 0.078125
- out_grad: bfloat16 [256, 12288], P('row', 'col'), may hold values from -6 to 6
- block_mask: int32 [96, 192], replicated, may hold values from 0 to 1, as said below
Outputs:
- outputs: bfloat16 [256, 12288], P('row', 'col')
- in_grad: bfloat16 [256, 12288], P('row', 'col')
- up_grad: bfloat16 [12288, 24576], P('col', 'row')
- down_grad: bfloat16 [24576, 12288], P('row', 'col')
The draws below stay inside these ranges and needn't reach their ends.
Inputs may be any that keep to these rules, and one draw needn't show every extreme that they name: `block_mask`: 1 marks a kept block: block (i, j) of up_weight and block (j, i) of down_weight; 0 marks a block that is zero. The kept blocks are the union of a butterfly pattern (rows and columns each carry a 5-bit code; block (i, j) is kept when the codes of i and j differ in at most one bit), 3 full block rows and 6 full block columns.
All inputs are finite; a program needn't handle non-finite values.
Results may differ from the reference program's by a relative error of at most 0.005.
Values may be sent and summed in bfloat16 or wider, within the bound.
No kernel may reach another device: no remote copies, remote signals or barrier semaphores. Data moves between devices by JAX's collectives and lax.ppermute only.
A program may use at most 64 MiB of HBM per device.

```python
import jax
import jax.numpy as jnp

D = 12288
FF = 24576
BLK = 128
TOKENS = 256


def draw_block_mask(key, part):
    key = jax.random.fold_in(key, 11)
    keys = jax.random.split(key, 4)
    row_count = D // BLK
    col_count = FF // BLK
    rows_perm = jax.random.permutation(keys[0], row_count).astype(jnp.int32)
    cols_perm = jax.random.permutation(keys[1], col_count).astype(jnp.int32)
    differ = jnp.bitwise_xor((rows_perm % 32)[:, None], (cols_perm % 32)[None, :])
    ones_count = sum([jnp.bitwise_and(jnp.right_shift(differ, shift_by), 1) for shift_by in range(5)])
    butterfly = ones_count <= 1
    global_rows = jax.random.permutation(keys[2], row_count).astype(jnp.int32) < max(1, row_count // 32)
    global_cols = jax.random.permutation(keys[3], col_count).astype(jnp.int32) < max(1, col_count // 32)
    kept = jnp.logical_or(butterfly, jnp.logical_or(global_rows[:, None], global_cols[None, :]))
    return kept.astype(jnp.int32)


def steps_of(own_key, dims, pieces, smallest, largest):
    level, own = 1.0, jax.random.fold_in(own_key, 6)
    for dim, shards_of in pieces:
        steps = jnp.exp(jax.random.uniform(jax.random.fold_in(own, dim), (shards_of,), jnp.float32, smallest / len(pieces), largest / len(pieces)))
        level = level * jnp.repeat(steps, dims[dim] // shards_of).reshape([-1 if axis == dim else 1 for axis in range(len(dims))])
    return level


def noise(key, shape, deviation, most, shards=(), dtype=jnp.bfloat16):
    entries = deviation * jax.random.normal(key, shape, jnp.float32)
    if shards:
        entries = entries * steps_of(key, shape, shards, -0.22, 0.18)
    return jnp.clip(entries, -most, most).astype(dtype)


def setup_inputs(seed: int = 0) -> dict:
    arg_keys = jax.random.split(jax.random.key(seed), 6)
    inputs = noise(arg_keys[0], (TOKENS, D), 1.0, 6.0, ((0, 64), (1, 8)))
    up_weight = noise(arg_keys[1], (D, FF), (D // 4) ** -0.5, 0.109375, ((0, 8), (1, 64)))
    down_weight = noise(arg_keys[2], (FF, D), (FF // 4) ** -0.5, 0.078125, ((0, 64), (1, 8)))
    out_grad = noise(arg_keys[3], (TOKENS, D), 1.0, 6.0, ((0, 64), (1, 8)))
    block_mask = draw_block_mask(jax.random.fold_in(arg_keys[5], 71), 0)
    return {"inputs": inputs, "up_weight": up_weight, "down_weight": down_weight, "out_grad": out_grad, "block_mask": block_mask}


slope_coef = 0.7978845608
cubic_coef = 0.044715


def gelu_value(values):
    tangent = jnp.tanh(slope_coef * (values + cubic_coef * values * values * values))
    return 0.5 * values * (1.0 + tangent)


def gelu_slope(values):
    tangent = jnp.tanh(slope_coef * (values + cubic_coef * values * values * values))
    return 0.5 * (1.0 + tangent) + 0.5 * values * (1.0 - tangent * tangent) * slope_coef * (1.0 + 3.0 * cubic_coef * values * values)


def apply_blocks(matrix, blocks):
    rows_b, cols_b = blocks.shape
    shaped = matrix.reshape(rows_b, BLK, cols_b, BLK) * blocks[:, None, :, None]
    return shaped.reshape(matrix.shape)


def reference(inputs, up_weight, down_weight, out_grad, block_mask):
    half_blocks = block_mask.astype(jnp.bfloat16)
    full_blocks = block_mask.astype(jnp.float32)
    up_masked = apply_blocks(up_weight, half_blocks)
    down_masked = apply_blocks(down_weight, half_blocks.T)
    hidden = jnp.dot(inputs, up_masked, preferred_element_type=jnp.float32)
    activation = gelu_value(hidden).astype(jnp.bfloat16)
    outputs = jnp.dot(activation, down_masked, preferred_element_type=jnp.float32).astype(jnp.bfloat16)
    grad_hidden = jnp.dot(out_grad, down_masked.T, preferred_element_type=jnp.float32)
    act_grad = (grad_hidden * gelu_slope(hidden)).astype(jnp.bfloat16)
    down_grad = apply_blocks(jnp.dot(activation.T, out_grad, preferred_element_type=jnp.float32), full_blocks.T).astype(jnp.bfloat16)
    up_grad = apply_blocks(jnp.dot(inputs.T, act_grad, preferred_element_type=jnp.float32), full_blocks).astype(jnp.bfloat16)
    in_grad = jnp.dot(act_grad, up_masked.T, preferred_element_type=jnp.float32).astype(jnp.bfloat16)
    return (outputs, in_grad, up_grad, down_grad)
```

```python
import jax
import jax.numpy as jnp
from jax import lax
from jax.sharding import Mesh, PartitionSpec as P

BLK = 128
AXES = ("zh", "zl", "x", "yh", "yl", "core")
SIZES = (4, 2, 4, 2, 4, 2)
ROW = ("zh", "zl", "x", "yh")
COL = ("yl", "core")
FAR = ("zh", "yh")
NEAR = ("x", "zl")

slope_coef = 0.7978845608
cubic_coef = 0.044715


def gelu_pair(values):
    tangent = jnp.tanh(slope_coef * (values + cubic_coef * values * values * values))
    value = 0.5 * values * (1.0 + tangent)
    slope = 0.5 * (1.0 + tangent) + 0.5 * values * (1.0 - tangent * tangent) * slope_coef * (
        1.0 + 3.0 * cubic_coef * values * values
    )
    return value, slope


def apply_blocks(matrix, blocks):
    rows_b, cols_b = blocks.shape
    shaped = (
        matrix.reshape(rows_b, BLK, cols_b, BLK) * blocks.astype(matrix.dtype)[:, None, :, None]
    )
    return shaped.reshape(matrix.shape)


def spread(block, axes, count):
    copies = jnp.broadcast_to(block[None], (count,) + block.shape)
    return lax.all_to_all(copies, axes, split_axis=0, concat_axis=0, tiled=True)


def swap(blocks, axes):
    return lax.all_to_all(blocks, axes, split_axis=0, concat_axis=0, tiled=True)


def local(inputs, up_weight, down_weight, out_grad, block_mask):
    row_index = lax.axis_index(ROW)
    col_index = lax.axis_index(COL)
    core = lax.axis_index("core")
    rows, width = inputs.shape
    units = up_weight.shape[1]
    d_blocks = width // BLK
    f_blocks = units // BLK
    local_mask = lax.dynamic_slice(
        block_mask, (col_index * d_blocks, row_index * f_blocks), (d_blocks, f_blocks)
    )
    down_mask = local_mask.T
    up_masked = apply_blocks(up_weight, local_mask)
    down_masked = apply_blocks(down_weight, down_mask)

    both = jnp.stack([inputs, out_grad])
    far = spread(both, FAR, 8)
    far = far.transpose(1, 0, 2, 3).reshape(2, 8 * rows, width)
    near = spread(far, NEAR, 8)
    tokens = 64 * rows
    panel_in = near[:, 0].reshape(tokens, width)
    panel_grad = near[:, 1].reshape(tokens, width)

    part_hidden = jnp.dot(panel_in, up_masked, preferred_element_type=jnp.float32)
    part_grad = lax.dot_general(
        panel_grad, down_masked, (((1,), (1,)), ((), ())), preferred_element_type=jnp.float32
    )
    half = tokens // 2
    parts = jnp.stack([part_hidden, part_grad]).reshape(2, 2, half, units)
    keep = jnp.where(core == 0, parts[:, 0], parts[:, 1])
    give = jnp.where(core == 0, parts[:, 1], parts[:, 0]).astype(jnp.bfloat16)
    got = lax.ppermute(give, "core", [(0, 1), (1, 0)])
    pair = (keep + got.astype(jnp.float32)).astype(jnp.bfloat16)
    quarter = half // 4
    pair = pair.reshape(2, 4, quarter, units).transpose(1, 0, 2, 3)
    summed = jnp.sum(swap(pair, "yl").astype(jnp.float32), axis=0)
    value, slope = gelu_pair(summed[0])
    acts = jnp.stack([value, summed[1] * slope]).astype(jnp.bfloat16)
    acts = spread(acts, "yl", 4)
    acts = acts.transpose(1, 0, 2, 3).reshape(1, 2, half, units)
    acts = lax.all_gather(acts, "core", axis=0, tiled=True)
    full_act = acts[:, 0].reshape(tokens, units)
    full_dact = acts[:, 1].reshape(tokens, units)

    out_terms = jnp.dot(full_act, down_masked, preferred_element_type=jnp.float32)
    in_terms = lax.dot_general(
        full_dact, up_masked, (((1,), (1,)), ((), ())), preferred_element_type=jnp.float32
    )
    down_full = lax.dot_general(
        full_act, panel_grad, (((0,), (0,)), ((), ())), preferred_element_type=jnp.float32
    )
    down_grad = apply_blocks(down_full, down_mask).astype(jnp.bfloat16)
    up_full = lax.dot_general(
        panel_in, full_dact, (((0,), (0,)), ((), ())), preferred_element_type=jnp.float32
    )
    up_grad = apply_blocks(up_full, local_mask).astype(jnp.bfloat16)

    terms = jnp.stack([out_terms, in_terms]).astype(jnp.bfloat16)
    terms = terms.reshape(2, 8, 8 * rows, width).transpose(1, 0, 2, 3)
    sums = jnp.sum(swap(terms, NEAR).astype(jnp.float32), axis=0).astype(jnp.bfloat16)
    sums = sums.reshape(2, 8, rows, width).transpose(1, 0, 2, 3)
    totals = jnp.sum(swap(sums, FAR).astype(jnp.float32), axis=0).astype(jnp.bfloat16)
    return (totals[0], totals[1], up_grad, down_grad)


def solution(mesh):
    fine = Mesh(mesh.devices.reshape(SIZES), AXES)
    in_specs = (P(ROW, COL), P(COL, ROW), P(ROW, COL), P(ROW, COL), P())
    out_specs = (P(ROW, COL), P(ROW, COL), P(COL, ROW), P(ROW, COL))
    return jax.shard_map(local, mesh=fine, in_specs=in_specs, out_specs=out_specs, check_vma=False)
```

```python
import jax
import jax.numpy as jnp
from jax import lax
from jax.experimental import pallas as pl
from jax.experimental.pallas import tpu as pltpu
from jax.sharding import Mesh, PartitionSpec as P

BLK = 128
AXES = ("zh", "zl", "x", "yh", "yl", "core")
SIZES = (4, 2, 4, 2, 4, 2)
ROW = ("zh", "zl", "x", "yh")
COL = ("yl", "core")
FAR = ("zh", "yh")
NEAR = ("x", "zl")
STEPS = 3

slope_coef = 0.7978845608
cubic_coef = 0.044715


def gelu_pair(values):
    tangent = jnp.tanh(slope_coef * (values + cubic_coef * values * values * values))
    value = 0.5 * values * (1.0 + tangent)
    slope = 0.5 * (1.0 + tangent) + 0.5 * values * (1.0 - tangent * tangent) * slope_coef * (
        1.0 + 3.0 * cubic_coef * values * values
    )
    return value, slope


def spread(block, axes, count):
    copies = jnp.broadcast_to(block[None], (count,) + block.shape)
    return lax.all_to_all(copies, axes, split_axis=0, concat_axis=0, tiled=True)


def swap(blocks, axes):
    return lax.all_to_all(blocks, axes, split_axis=0, concat_axis=0, tiled=True)


def kept(mask_ref, d_block, f_block, block):
    return jnp.where(mask_ref[d_block, f_block] != 0, block, jnp.zeros_like(block))


def mask_weights(step, mask_ref, up_ref, down_ref, um, dm):
    wide, units = um.shape
    for i in range(wide // BLK):
        d = slice(i * BLK, (i + 1) * BLK)
        for j in range(units // BLK):
            f = slice(j * BLK, (j + 1) * BLK)
            d_block = step * (wide // BLK) + i
            um[d, f] = kept(mask_ref, d_block, j, up_ref[d, f])
            dm[f, d] = kept(mask_ref, d_block, j, down_ref[f, d])


def first_kernel(core_ref, mask_ref, near_ref, up_ref, down_ref, keep_ref, give_ref, um, dm, hid, grd):
    step = pl.program_id(0)
    mask_weights(step, mask_ref, up_ref, down_ref, um, dm)
    tokens, wide = hid.shape[0], um.shape[0]
    x = near_ref[:, 0].reshape(tokens, wide)
    g = near_ref[:, 1].reshape(tokens, wide)
    h = jnp.dot(x, um[...], preferred_element_type=jnp.float32)
    q = lax.dot_general(g, dm[...], (((1,), (1,)), ((), ())), preferred_element_type=jnp.float32)

    @pl.when(step == 0)
    def _():
        hid[...] = h
        grd[...] = q

    @pl.when(step > 0)
    def _():
        hid[...] += h
        grd[...] += q

    @pl.when(step == pl.num_programs(0) - 1)
    def _():
        half = tokens // 2
        low = core_ref[0] == 0
        for k, acc in enumerate((hid, grd)):
            a, b = acc[:half], acc[half:]
            keep_ref[k] = jnp.where(low, a, b)
            give_ref[k] = jnp.where(low, b, a).astype(give_ref.dtype)


def second_kernel(mask_ref, acts_ref, up_ref, down_ref, terms_ref, um, dm):
    step = pl.program_id(0)
    mask_weights(step, mask_ref, up_ref, down_ref, um, dm)
    blocks, _, rows, units = acts_ref.shape
    wide = um.shape[0]
    act = acts_ref[:, 0].reshape(blocks * rows, units)
    dact = acts_ref[:, 1].reshape(blocks * rows, units)
    out = jnp.dot(act, dm[...], preferred_element_type=jnp.float32)
    terms_ref[:, 0] = out.astype(terms_ref.dtype).reshape(blocks, rows, wide)
    back = lax.dot_general(dact, um[...], (((1,), (1,)), ((), ())), preferred_element_type=jnp.float32)
    terms_ref[:, 1] = back.astype(terms_ref.dtype).reshape(blocks, rows, wide)


def third_kernel(mask_ref, acts_ref, near_ref, upg_ref, downg_ref):
    step = pl.program_id(0)
    blocks, _, rows, units = acts_ref.shape
    wide = upg_ref.shape[0]
    tokens = blocks * rows
    act = acts_ref[:, 0].reshape(tokens, units)
    dact = acts_ref[:, 1].reshape(tokens, units)
    x = near_ref[:, 0].reshape(tokens, wide)
    g = near_ref[:, 1].reshape(tokens, wide)
    lead = (((0,), (0,)), ((), ()))
    down = lax.dot_general(act, g, lead, preferred_element_type=jnp.float32).astype(downg_ref.dtype)
    up = lax.dot_general(x, dact, lead, preferred_element_type=jnp.float32).astype(upg_ref.dtype)
    for i in range(wide // BLK):
        d = slice(i * BLK, (i + 1) * BLK)
        for j in range(units // BLK):
            f = slice(j * BLK, (j + 1) * BLK)
            d_block = step * (wide // BLK) + i
            upg_ref[d, f] = kept(mask_ref, d_block, j, up[d, f])
            downg_ref[f, d] = kept(mask_ref, d_block, j, down[f, d])


def local(inputs, up_weight, down_weight, out_grad, block_mask):
    row_index = lax.axis_index(ROW)
    col_index = lax.axis_index(COL)
    core = lax.axis_index("core")
    rows, width = inputs.shape
    units = up_weight.shape[1]
    d_blocks = width // BLK
    f_blocks = units // BLK
    tokens = 64 * rows
    half = tokens // 2
    quarter = half // 4
    wide = width // STEPS
    bf, f4 = jnp.bfloat16, jnp.float32
    smem = pl.BlockSpec(memory_space=pltpu.SMEM)
    near_spec = pl.BlockSpec((8, 2, 8 * rows, wide), lambda k: (0, 0, 0, k))
    acts_spec = pl.BlockSpec((8, 2, quarter, units), lambda k: (0, 0, 0, 0))
    up_spec = pl.BlockSpec((wide, units), lambda k: (k, 0))
    down_spec = pl.BlockSpec((units, wide), lambda k: (0, k))
    half_spec = pl.BlockSpec((2, half, units), lambda k: (0, 0, 0))
    masked = [pltpu.VMEM((wide, units), bf), pltpu.VMEM((units, wide), bf)]
    flops = 2 * 2 * tokens * width * units
    weight_bytes = 2 * 2 * width * units
    panel_bytes = 2 * 2 * tokens * width

    mask = lax.dynamic_slice(
        block_mask, (col_index * d_blocks, row_index * f_blocks), (d_blocks, f_blocks)
    )

    both = jnp.stack([inputs, out_grad])
    far = spread(both, FAR, 8)
    far, mask = lax.optimization_barrier((far, mask))
    far = far.transpose(1, 0, 2, 3).reshape(2, 8 * rows, width)
    near = spread(far, NEAR, 8)

    keep, give = pl.pallas_call(
        first_kernel,
        grid=(STEPS,),
        in_specs=[smem, smem, near_spec, up_spec, down_spec],
        out_specs=[half_spec, half_spec],
        out_shape=[
            jax.ShapeDtypeStruct((2, half, units), f4),
            jax.ShapeDtypeStruct((2, half, units), f4),
        ],
        scratch_shapes=masked + [pltpu.VMEM((tokens, units), f4)] * 2,
        cost_estimate=pl.CostEstimate(
            flops=flops, bytes_accessed=weight_bytes + panel_bytes, transcendentals=0
        ),
        name="partial_sums",
    )(core.reshape(1), mask, near, up_weight, down_weight)
    got = lax.ppermute(give, "core", [(0, 1), (1, 0)])
    pair = (keep + got).reshape(2, 4, quarter, units).transpose(1, 0, 2, 3)
    summed = jnp.sum(swap(pair, "yl"), axis=0)
    value, slope = gelu_pair(summed[0])
    acts = jnp.stack([value, summed[1] * slope]).astype(bf)
    acts = spread(acts, "yl", 4)
    acts = acts.reshape(1, 8 * quarter, units)
    acts = lax.all_gather(acts, "core", axis=0, tiled=True).reshape(8, 2, quarter, units)

    terms = pl.pallas_call(
        second_kernel,
        grid=(STEPS,),
        in_specs=[smem, acts_spec, up_spec, down_spec],
        out_specs=near_spec,
        out_shape=jax.ShapeDtypeStruct((8, 2, 8 * rows, width), bf),
        scratch_shapes=masked,
        cost_estimate=pl.CostEstimate(
            flops=flops, bytes_accessed=weight_bytes + panel_bytes, transcendentals=0
        ),
        name="output_terms",
    )(mask, acts, up_weight, down_weight)

    terms = swap(terms, NEAR)
    terms, acts, near = lax.optimization_barrier((terms, acts, near))
    sums = jnp.sum(terms.astype(f4), axis=0).astype(bf)
    sums = sums.reshape(2, 8, rows, width).transpose(1, 0, 2, 3)
    sums = swap(sums, FAR)
    up_grad, down_grad = pl.pallas_call(
        third_kernel,
        grid=(STEPS,),
        in_specs=[smem, acts_spec, near_spec],
        out_specs=[up_spec, down_spec],
        out_shape=[
            jax.ShapeDtypeStruct((width, units), bf),
            jax.ShapeDtypeStruct((units, width), bf),
        ],
        cost_estimate=pl.CostEstimate(
            flops=flops, bytes_accessed=weight_bytes + panel_bytes, transcendentals=0
        ),
        name="weight_grads",
    )(mask, acts, near)
    sums, up_grad, down_grad = lax.optimization_barrier((sums, up_grad, down_grad))
    totals = jnp.sum(sums.astype(f4), axis=0).astype(bf)
    return (totals[0], totals[1], up_grad, down_grad)


def solution(mesh):
    fine = Mesh(mesh.devices.reshape(SIZES), AXES)
    in_specs = (P(ROW, COL), P(COL, ROW), P(ROW, COL), P(ROW, COL), P())
    out_specs = (P(ROW, COL), P(ROW, COL), P(COL, ROW), P(ROW, COL))
    return jax.shard_map(local, mesh=fine, in_specs=in_specs, out_specs=out_specs, check_vma=False)
```

```python
import jax
import jax.numpy as jnp
from jax import lax
from jax.experimental import pallas as pl
from jax.experimental.pallas import tpu as pltpu
from jax.sharding import Mesh, PartitionSpec as P

BLK = 128
AXES = ("zh", "zl", "xh", "xl", "yh", "ylh", "yll", "core")
SIZES = (4, 2, 2, 2, 2, 2, 2, 2)
ROW = ("zh", "zl", "xh", "xl", "yh")
COL = ("ylh", "yll", "core")
FAR = ("yh", "zh")
NEAR = ("xl", "xh", "zl")
LINE = ("yll", "ylh")
VMEM_BYTES = 16 * 1024 * 1024

slope_coef = 0.7978845608
cubic_coef = 0.044715


def gelu_pair(values):
    tangent = jnp.tanh(slope_coef * (values + cubic_coef * values * values * values))
    value = 0.5 * values * (1.0 + tangent)
    slope = 0.5 * (1.0 + tangent) + 0.5 * values * (1.0 - tangent * tangent) * slope_coef * (
        1.0 + 3.0 * cubic_coef * values * values
    )
    return value, slope


def spread(block, axes, count):
    copies = jnp.broadcast_to(block[None], (count,) + block.shape)
    return lax.all_to_all(copies, axes, split_axis=0, concat_axis=0, tiled=True)


def swap(blocks, axes):
    return lax.all_to_all(blocks, axes, split_axis=0, concat_axis=0, tiled=True)


def kept(mask_ref, d_block, f_block, block):
    return jnp.where(mask_ref[d_block, f_block] != 0, block, jnp.zeros_like(block))


def dot(a, b, axis_a, axis_b):
    dims = (((axis_a,), (axis_b,)), ((), ()))
    return lax.dot_general(a, b, dims, preferred_element_type=jnp.float32)


def first_kernel(core_ref, mask_ref, near_ref, up_ref, down_ref, keep_ref, give_ref, um, dm):
    width, units = um.shape
    for i in range(width // BLK):
        d = slice(i * BLK, (i + 1) * BLK)
        for j in range(units // BLK):
            f = slice(j * BLK, (j + 1) * BLK)
            um[d, f] = kept(mask_ref, i, j, up_ref[d, f])
            dm[f, d] = kept(mask_ref, i, j, down_ref[f, d])
    half = keep_ref.shape[1]
    hidden = dot(near_ref[:, 0].reshape(2 * half, width), um[...], 1, 0)
    grad = dot(near_ref[:, 1].reshape(2 * half, width), dm[...], 1, 1)
    low = core_ref[0] == 0
    for k, part in enumerate((hidden, grad)):
        a, b = part[:half], part[half:]
        keep_ref[k] = jnp.where(low, a, b)
        give_ref[k] = jnp.where(low, b, a)


def second_kernel(acts_ref, um, dm, terms_ref):
    blocks, _, rows, units = acts_ref.shape
    width = um.shape[0]
    wide = width // 3
    act = acts_ref[:, 0].reshape(blocks * rows, units)
    dact = acts_ref[:, 1].reshape(blocks * rows, units)
    for k in range(3):
        w = slice(k * wide, (k + 1) * wide)
        out = dot(act, dm[:, w], 1, 0).astype(terms_ref.dtype)
        terms_ref[:, 0, :, w] = out.reshape(blocks, rows, wide)
        back = dot(dact, um[w, :], 1, 1).astype(terms_ref.dtype)
        terms_ref[:, 1, :, w] = back.reshape(blocks, rows, wide)


def third_kernel(mask_ref, acts_ref, near_ref, upg_ref, downg_ref):
    blocks, _, rows, units = acts_ref.shape
    width = upg_ref.shape[0]
    wide = width // 3
    tokens = blocks * rows
    act = acts_ref[:, 0].reshape(tokens, units)
    dact = acts_ref[:, 1].reshape(tokens, units)
    for k in range(3):
        w = slice(k * wide, (k + 1) * wide)
        down = dot(act, near_ref[:, 1, :, w].reshape(tokens, wide), 0, 0).astype(downg_ref.dtype)
        up = dot(near_ref[:, 0, :, w].reshape(tokens, wide), dact, 0, 0).astype(upg_ref.dtype)
        for i in range(wide // BLK):
            d = slice(i * BLK, (i + 1) * BLK)
            at = slice(k * wide + i * BLK, k * wide + (i + 1) * BLK)
            for j in range(units // BLK):
                f = slice(j * BLK, (j + 1) * BLK)
                d_block = k * (wide // BLK) + i
                upg_ref[at, f] = kept(mask_ref, d_block, j, up[d, f])
                downg_ref[f, at] = kept(mask_ref, d_block, j, down[f, d])


def local(inputs, up_weight, down_weight, out_grad, block_mask):
    row_index = lax.axis_index(ROW)
    col_index = lax.axis_index(COL)
    core = lax.axis_index("core")
    rows, width = inputs.shape
    units = up_weight.shape[1]
    d_blocks = width // BLK
    f_blocks = units // BLK
    tokens = 64 * rows
    half = tokens // 2
    quarter = half // 4
    bf, f4 = jnp.bfloat16, jnp.float32
    smem = pl.BlockSpec(memory_space=pltpu.SMEM)
    vmem = pl.BlockSpec(memory_space=pltpu.VMEM)
    params = pltpu.CompilerParams(vmem_limit_bytes=VMEM_BYTES)
    cost = pl.CostEstimate(
        flops=4 * tokens * width * units,
        bytes_accessed=4 * width * (units + tokens),
        transcendentals=0,
    )
    masked = [jax.ShapeDtypeStruct((width, units), bf), jax.ShapeDtypeStruct((units, width), bf)]

    both = jnp.stack([inputs, out_grad])
    far = spread(both, FAR, 8)
    mask = lax.dynamic_slice(
        block_mask, (col_index * d_blocks, row_index * f_blocks), (d_blocks, f_blocks)
    )
    far, mask = lax.optimization_barrier((far, mask))
    far = far.transpose(1, 0, 2, 3).reshape(2, 8 * rows, width)
    near = spread(far, NEAR, 8)

    keep, give, up_masked, down_masked = pl.pallas_call(
        first_kernel,
        in_specs=[smem, smem, vmem, vmem, vmem],
        out_specs=[vmem] * 4,
        out_shape=[jax.ShapeDtypeStruct((2, half, units), f4)] * 2 + masked,
        compiler_params=params,
        cost_estimate=cost,
        name="partial_sums",
    )(core.reshape(1), mask, near, up_weight, down_weight)
    pair = keep + lax.ppermute(give, "core", [(0, 1), (1, 0)])
    pair = pair.reshape(2, 4, quarter, units).transpose(1, 0, 2, 3)
    sent = pair.astype(bf)
    lost = lax.dynamic_index_in_dim(pair, lax.axis_index(LINE), 0, keepdims=False)
    lost = lost - lost.astype(bf).astype(f4)
    sent, lost = lax.optimization_barrier((sent, lost))
    summed = jnp.sum(swap(sent, LINE).astype(f4), axis=0) + lost
    value, slope = gelu_pair(summed[0])
    acts = jnp.stack([value, summed[1] * slope]).astype(bf)
    acts = spread(acts, LINE, 4).reshape(1, 8 * quarter, units)
    acts = lax.all_gather(acts, "core", axis=0, tiled=True).reshape(8, 2, quarter, units)

    terms = pl.pallas_call(
        second_kernel,
        in_specs=[vmem] * 3,
        out_specs=vmem,
        out_shape=jax.ShapeDtypeStruct((8, 2, 8 * rows, width), bf),
        compiler_params=params,
        cost_estimate=cost,
        name="output_terms",
    )(acts, up_masked, down_masked)

    terms = swap(terms, NEAR)
    terms, acts, near = lax.optimization_barrier((terms, acts, near))
    sums = jnp.sum(terms.astype(f4), axis=0).astype(bf)
    sums = sums.reshape(2, 8, rows, width).transpose(1, 0, 2, 3)
    sums, acts, near = lax.optimization_barrier((sums, acts, near))
    sums = swap(sums, FAR)
    up_grad, down_grad = pl.pallas_call(
        third_kernel,
        in_specs=[smem, vmem, vmem],
        out_specs=[vmem, vmem],
        out_shape=masked,
        compiler_params=params,
        cost_estimate=cost,
        name="weight_grads",
    )(mask, acts, near)
    sums, up_grad, down_grad = lax.optimization_barrier((sums, up_grad, down_grad))
    totals = jnp.sum(sums.astype(f4), axis=0).astype(bf)
    return (totals[0], totals[1], up_grad, down_grad)


def solution(mesh):
    fine = Mesh(mesh.devices.reshape(SIZES), AXES)
    in_specs = (P(ROW, COL), P(COL, ROW), P(ROW, COL), P(ROW, COL), P())
    out_specs = (P(ROW, COL), P(ROW, COL), P(COL, ROW), P(ROW, COL))
    return jax.shard_map(local, mesh=fine, in_specs=in_specs, out_specs=out_specs, check_vma=False)
```

```python
import math

import jax
import jax.numpy as jnp
import numpy as np
from jax import lax
from jax.experimental import pallas as pl
from jax.experimental.pallas import tpu as pltpu
from jax.sharding import Mesh, PartitionSpec as P

BLK = 128
AXES = ("zh", "zl", "xh", "xl", "yh", "ylh", "yll", "core")
SIZES = (4, 2, 2, 2, 2, 2, 2, 2)
ROW = ("zh", "zl", "xh", "xl", "yh")
COL = ("ylh", "yll", "core")
FAR = ("xh", "zh", "yh")
FARS = 16
NEARS = 4
LINE = ("yll", "ylh")
VMEM_BYTES = 10 * 1024 * 1024

slope_coef = 0.7978845608
cubic_coef = 0.044715


def gelu_pair(values):
    tangent = jnp.tanh(slope_coef * (values + cubic_coef * values * values * values))
    value = 0.5 * values * (1.0 + tangent)
    slope = 0.5 * (1.0 + tangent) + 0.5 * values * (1.0 - tangent * tangent) * slope_coef * (
        1.0 + 3.0 * cubic_coef * values * values
    )
    return value, slope


def near_groups():
    order = np.arange(math.prod(SIZES)).reshape(8, 4, 2, 4, 2)
    groups = []
    for yh, yl, core, zp, xp in np.ndindex(2, 4, 2, 4, 2):
        zs = sorted(((2 * zp + core) % 8, (2 * zp + core + 1) % 8), key=lambda z: z % 2)
        xs = sorted(((2 * xp + core) % 4, (2 * xp + core + 1) % 4), key=lambda x: x % 2)
        groups.append([int(order[z, x, yh, yl, core]) for x in xs for z in zs])
    return groups


def near_swap(blocks):
    return lax.all_to_all(
        blocks, AXES, split_axis=0, concat_axis=0, tiled=True, axis_index_groups=near_groups()
    )


def spread(block, axes, count):
    copies = jnp.broadcast_to(block[None], (count,) + block.shape)
    return lax.all_to_all(copies, axes, split_axis=0, concat_axis=0, tiled=True)


def swap(blocks, axes):
    return lax.all_to_all(blocks, axes, split_axis=0, concat_axis=0, tiled=True)


def kept(mask_ref, d_block, f_block, block):
    return jnp.where(mask_ref[d_block, f_block] != 0, block, jnp.zeros_like(block))


def dot(a, b, axis_a, axis_b):
    dims = (((axis_a,), (axis_b,)), ((), ()))
    return lax.dot_general(a, b, dims, preferred_element_type=jnp.float32)


def mask_weights(mask_ref, up_ref, down_ref, um, dm):
    width, units = um.shape
    for i in range(width // BLK):
        d = slice(i * BLK, (i + 1) * BLK)
        for j in range(units // BLK):
            f = slice(j * BLK, (j + 1) * BLK)
            um[d, f] = kept(mask_ref, i, j, up_ref[d, f])
            dm[f, d] = kept(mask_ref, i, j, down_ref[f, d])


def first_kernel(
    core_ref, mask_ref, near_ref, up_ref, down_ref, keep_ref, give_ref, saved_ref, um, dm, sem
):
    saving = pltpu.make_async_copy(near_ref, saved_ref, sem)
    saving.start()
    mask_weights(mask_ref, up_ref, down_ref, um, dm)
    width = um.shape[0]
    half = keep_ref.shape[1]
    hidden = dot(near_ref[:, 0].reshape(2 * half, width), um[...], 1, 0)
    grad = dot(near_ref[:, 1].reshape(2 * half, width), dm[...], 1, 1)
    low = core_ref[0] == 0
    for k, part in enumerate((hidden, grad)):
        a, b = part[:half], part[half:]
        keep_ref[k] = jnp.where(low, a, b)
        give_ref[k] = jnp.where(low, b, a)
    saving.wait()


def second_kernel(mask_ref, acts_ref, up_ref, down_ref, terms_ref, um, dm):
    mask_weights(mask_ref, up_ref, down_ref, um, dm)
    blocks, _, rows, units = acts_ref.shape
    width = um.shape[0]
    wide = width // 3
    act = acts_ref[:, 0].reshape(blocks * rows, units)
    dact = acts_ref[:, 1].reshape(blocks * rows, units)
    blocks, _, rows, _ = terms_ref.shape
    for k in range(3):
        w = slice(k * wide, (k + 1) * wide)
        out = dot(act, dm[:, w], 1, 0).astype(terms_ref.dtype)
        terms_ref[:, 0, :, w] = out.reshape(blocks, rows, wide)
        back = dot(dact, um[w, :], 1, 1).astype(terms_ref.dtype)
        terms_ref[:, 1, :, w] = back.reshape(blocks, rows, wide)


def third_kernel(mask_ref, acts_ref, near_ref, upg_ref, downg_ref):
    blocks, _, rows, units = acts_ref.shape
    width = upg_ref.shape[0]
    wide = width // 3
    tokens = blocks * rows
    act = acts_ref[:, 0].reshape(tokens, units)
    dact = acts_ref[:, 1].reshape(tokens, units)
    for k in range(3):
        w = slice(k * wide, (k + 1) * wide)
        down = dot(act, near_ref[:, 1, :, w].reshape(tokens, wide), 0, 0).astype(downg_ref.dtype)
        up = dot(near_ref[:, 0, :, w].reshape(tokens, wide), dact, 0, 0).astype(upg_ref.dtype)
        for i in range(wide // BLK):
            d = slice(i * BLK, (i + 1) * BLK)
            at = slice(k * wide + i * BLK, k * wide + (i + 1) * BLK)
            for j in range(units // BLK):
                f = slice(j * BLK, (j + 1) * BLK)
                d_block = k * (wide // BLK) + i
                upg_ref[at, f] = kept(mask_ref, d_block, j, up[d, f])
                downg_ref[f, at] = kept(mask_ref, d_block, j, down[f, d])


def local(inputs, up_weight, down_weight, out_grad, block_mask):
    row_index = lax.axis_index(ROW)
    col_index = lax.axis_index(COL)
    core = lax.axis_index("core")
    rows, width = inputs.shape
    units = up_weight.shape[1]
    d_blocks = width // BLK
    f_blocks = units // BLK
    tokens = 64 * rows
    half = tokens // 2
    quarter = half // 4
    bf, f4 = jnp.bfloat16, jnp.float32
    smem = pl.BlockSpec(memory_space=pltpu.SMEM)
    vmem = pl.BlockSpec(memory_space=pltpu.VMEM)
    params = pltpu.CompilerParams(vmem_limit_bytes=VMEM_BYTES)
    cost = pl.CostEstimate(
        flops=4 * tokens * width * units,
        bytes_accessed=4 * width * (units + tokens),
        transcendentals=0,
    )
    scratch = [pltpu.VMEM((width, units), bf), pltpu.VMEM((units, width), bf)]
    masked = [jax.ShapeDtypeStruct((width, units), bf), jax.ShapeDtypeStruct((units, width), bf)]

    both = jnp.stack([inputs, out_grad])
    far = spread(both, FAR, FARS)
    mask = lax.dynamic_slice(
        block_mask, (col_index * d_blocks, row_index * f_blocks), (d_blocks, f_blocks)
    )
    far, mask = lax.optimization_barrier((far, mask))
    far = far.transpose(1, 0, 2, 3).reshape(1, 2, FARS * rows, width)
    near = near_swap(jnp.broadcast_to(far, (NEARS,) + far.shape[1:]))

    keep, give, saved = pl.pallas_call(
        first_kernel,
        in_specs=[smem, smem, vmem, vmem, vmem],
        out_specs=[vmem, vmem, pl.BlockSpec(memory_space=pltpu.HBM)],
        out_shape=[jax.ShapeDtypeStruct((2, half, units), f4)] * 2
        + [jax.ShapeDtypeStruct(near.shape, bf)],
        scratch_shapes=scratch + [pltpu.SemaphoreType.DMA],
        compiler_params=params,
        cost_estimate=cost,
        name="partial_sums",
    )(core.reshape(1), mask, near, up_weight, down_weight)
    pair = keep + lax.ppermute(give, "core", [(0, 1), (1, 0)])
    pair = pair.reshape(2, 4, quarter, units).transpose(1, 0, 2, 3)
    sent = pair.astype(bf)
    lost = lax.dynamic_index_in_dim(pair, lax.axis_index(LINE), 0, keepdims=False)
    lost = lost - lost.astype(bf).astype(f4)
    sent, lost = lax.optimization_barrier((sent, lost))
    summed = jnp.sum(swap(sent, LINE).astype(f4), axis=0) + lost
    value, slope = gelu_pair(summed[0])
    acts = jnp.stack([value, summed[1] * slope]).astype(bf)
    acts = spread(acts, LINE, 4).reshape(1, 8 * quarter, units)
    acts = lax.all_gather(acts, "core", axis=0, tiled=True).reshape(8, 2, quarter, units)

    terms = pl.pallas_call(
        second_kernel,
        in_specs=[smem, vmem, vmem, vmem],
        out_specs=vmem,
        out_shape=jax.ShapeDtypeStruct((NEARS, 2, FARS * rows, width), bf),
        scratch_shapes=scratch,
        compiler_params=params,
        cost_estimate=cost,
        name="output_terms",
    )(mask, acts, up_weight, down_weight)

    terms = near_swap(terms)
    terms, acts, saved = lax.optimization_barrier((terms, acts, saved))
    sums = jnp.sum(terms.astype(f4), axis=0).astype(bf)
    sums = sums.reshape(2, FARS, rows, width).transpose(1, 0, 2, 3)
    sums, acts, saved = lax.optimization_barrier((sums, acts, saved))
    sums = swap(sums, FAR)
    up_grad, down_grad = pl.pallas_call(
        third_kernel,
        in_specs=[smem, vmem, vmem],
        out_specs=[vmem, vmem],
        out_shape=masked,
        compiler_params=params,
        cost_estimate=cost,
        name="weight_grads",
    )(mask, acts, saved)
    sums, up_grad, down_grad = lax.optimization_barrier((sums, up_grad, down_grad))
    totals = jnp.sum(sums.astype(f4), axis=0).astype(bf)
    return (totals[0], totals[1], up_grad, down_grad)


def solution(mesh):
    fine = Mesh(mesh.devices.reshape(SIZES), AXES)
    in_specs = (P(ROW, COL), P(COL, ROW), P(ROW, COL), P(ROW, COL), P())
    out_specs = (P(ROW, COL), P(ROW, COL), P(COL, ROW), P(ROW, COL))
    return jax.shard_map(local, mesh=fine, in_specs=in_specs, out_specs=out_specs, check_vma=False)
```

```python
import math

import jax
import jax.numpy as jnp
import numpy as np
from jax import lax
from jax.experimental import pallas as pl
from jax.experimental.pallas import tpu as pltpu
from jax.sharding import Mesh, PartitionSpec as P

BLK = 128
AXES = ("zh", "zl", "xh", "xl", "yh", "ylh", "yll", "core")
SIZES = (4, 2, 2, 2, 2, 2, 2, 2)
ROW = ("zh", "zl", "xh", "xl", "yh")
COL = ("ylh", "yll", "core")
FAR = ("xh", "zh", "yh")
FARS = 16
NEARS = 4
LINE = ("yll", "ylh")
VMEM_BYTES = 12 * 1024 * 1024
LARGE_VMEM_BYTES = 56 * 1024 * 1024

slope_coef = 0.7978845608
cubic_coef = 0.044715


def gelu_pair(values):
    tangent = jnp.tanh(slope_coef * (values + cubic_coef * values * values * values))
    value = 0.5 * values * (1.0 + tangent)
    slope = 0.5 * (1.0 + tangent) + 0.5 * values * (1.0 - tangent * tangent) * slope_coef * (
        1.0 + 3.0 * cubic_coef * values * values
    )
    return value, slope


def near_groups():
    order = np.arange(math.prod(SIZES)).reshape(8, 4, 2, 4, 2)
    groups = []
    for yh, yl, core, zp, xp in np.ndindex(2, 4, 2, 4, 2):
        zs = sorted(((2 * zp + core) % 8, (2 * zp + core + 1) % 8), key=lambda z: z % 2)
        xs = sorted(((2 * xp + core) % 4, (2 * xp + core + 1) % 4), key=lambda x: x % 2)
        groups.append([int(order[z, x, yh, yl, core]) for x in xs for z in zs])
    return groups


def near_swap(blocks):
    return lax.all_to_all(
        blocks, AXES, split_axis=0, concat_axis=0, tiled=True, axis_index_groups=near_groups()
    )


def spread(block, axes, count):
    copies = jnp.broadcast_to(block[None], (count,) + block.shape)
    return lax.all_to_all(copies, axes, split_axis=0, concat_axis=0, tiled=True)


def swap(blocks, axes):
    return lax.all_to_all(blocks, axes, split_axis=0, concat_axis=0, tiled=True)


def kept(mask_ref, d_block, f_block, block):
    return jnp.where(mask_ref[d_block, f_block] != 0, block, jnp.zeros_like(block))


def dot(a, b, axis_a, axis_b):
    dims = (((axis_a,), (axis_b,)), ((), ()))
    return lax.dot_general(a, b, dims, preferred_element_type=jnp.float32)


def mask_weights(mask_ref, up_ref, down_ref, um, dm):
    width, units = um.shape
    for i in range(width // BLK):
        d = slice(i * BLK, (i + 1) * BLK)
        for j in range(units // BLK):
            f = slice(j * BLK, (j + 1) * BLK)
            um[d, f] = kept(mask_ref, i, j, up_ref[d, f])
            dm[f, d] = kept(mask_ref, i, j, down_ref[f, d])


def first_kernel(
    core_ref, mask_ref, near_ref, up_ref, down_ref, keep_ref, give_ref, um, dm
):
    mask_weights(mask_ref, up_ref, down_ref, um, dm)
    width = um.shape[0]
    half = keep_ref.shape[1]
    hidden = dot(near_ref[:, :, :width].reshape(2 * half, width), um[...], 1, 0)
    grad = dot(near_ref[:, :, width:].reshape(2 * half, width), dm[...], 1, 1)
    low = core_ref[0] == 0
    for k, part in enumerate((hidden, grad)):
        a, b = part[:half], part[half:]
        keep_ref[k] = jnp.where(low, a, b)
        give_ref[k] = jnp.where(low, b, a)


def second_kernel(mask_ref, acts_ref, up_ref, down_ref, terms_ref, um, dm):
    mask_weights(mask_ref, up_ref, down_ref, um, dm)
    blocks, _, rows, units = acts_ref.shape
    width = um.shape[0]
    wide = width // 3
    act = acts_ref[:, 0].reshape(blocks * rows, units)
    dact = acts_ref[:, 1].reshape(blocks * rows, units)
    blocks, rows, _ = terms_ref.shape
    for k in range(3):
        w = slice(k * wide, (k + 1) * wide)
        out = dot(act, dm[:, w], 1, 0).astype(terms_ref.dtype)
        terms_ref[:, :, w] = out.reshape(blocks, rows, wide)
        back = dot(dact, um[w, :], 1, 1).astype(terms_ref.dtype)
        terms_ref[:, :, width + k * wide : width + (k + 1) * wide] = back.reshape(blocks, rows, wide)


def third_kernel(mask_ref, acts_ref, saved_ref, upg_ref, downg_ref, near_ref, sem):
    loading = [
        pltpu.make_async_copy(saved_ref.at[i], near_ref.at[i], sem.at[i])
        for i in range(near_ref.shape[0])
    ]
    for copy in loading:
        copy.start()
    for copy in loading:
        copy.wait()
    blocks, _, rows, units = acts_ref.shape
    width = upg_ref.shape[0]
    wide = width // 3
    tokens = blocks * rows
    act = acts_ref[:, 0].reshape(tokens, units)
    dact = acts_ref[:, 1].reshape(tokens, units)
    for k in range(3):
        w = slice(k * wide, (k + 1) * wide)
        g = near_ref[:, :, width + k * wide : width + (k + 1) * wide].reshape(tokens, wide)
        down = dot(act, g, 0, 0).astype(downg_ref.dtype)
        up = dot(near_ref[:, :, w].reshape(tokens, wide), dact, 0, 0).astype(upg_ref.dtype)
        for i in range(wide // BLK):
            d = slice(i * BLK, (i + 1) * BLK)
            at = slice(k * wide + i * BLK, k * wide + (i + 1) * BLK)
            for j in range(units // BLK):
                f = slice(j * BLK, (j + 1) * BLK)
                d_block = k * (wide // BLK) + i
                upg_ref[at, f] = kept(mask_ref, d_block, j, up[d, f])
                downg_ref[f, at] = kept(mask_ref, d_block, j, down[f, d])


def local(inputs, up_weight, down_weight, out_grad, block_mask):
    row_index = lax.axis_index(ROW)
    col_index = lax.axis_index(COL)
    core = lax.axis_index("core")
    rows, width = inputs.shape
    units = up_weight.shape[1]
    d_blocks = width // BLK
    f_blocks = units // BLK
    tokens = 64 * rows
    half = tokens // 2
    quarter = half // 4
    bf, f4 = jnp.bfloat16, jnp.float32
    smem = pl.BlockSpec(memory_space=pltpu.SMEM)
    vmem = pl.BlockSpec(memory_space=pltpu.VMEM)
    hbm = pl.BlockSpec(memory_space=pltpu.HBM)
    params = pltpu.CompilerParams(vmem_limit_bytes=VMEM_BYTES)
    cost = pl.CostEstimate(
        flops=4 * tokens * width * units,
        bytes_accessed=4 * width * (units + tokens),
        transcendentals=0,
    )
    scratch = [pltpu.VMEM((width, units), bf), pltpu.VMEM((units, width), bf)]
    masked = [jax.ShapeDtypeStruct((width, units), bf), jax.ShapeDtypeStruct((units, width), bf)]

    both = jnp.concatenate([inputs, out_grad], axis=1)
    far = spread(both, FAR, FARS)
    mask = lax.dynamic_slice(
        block_mask, (col_index * d_blocks, row_index * f_blocks), (d_blocks, f_blocks)
    )
    far, mask = lax.optimization_barrier((far, mask))
    far = far.reshape(1, FARS * rows, 2 * width)
    near = near_swap(jnp.broadcast_to(far, (NEARS,) + far.shape[1:]))

    keep, give = pl.pallas_call(
        first_kernel,
        in_specs=[smem, smem, vmem, vmem, vmem],
        out_specs=[vmem, vmem],
        out_shape=[jax.ShapeDtypeStruct((2, half, units), f4)] * 2,
        scratch_shapes=scratch,
        compiler_params=params,
        cost_estimate=cost,
        name="partial_sums",
    )(core.reshape(1), mask, near, up_weight, down_weight)
    pair = keep + lax.ppermute(give, "core", [(0, 1), (1, 0)])
    pair = pair.reshape(2, 4, quarter, units).transpose(1, 0, 2, 3)
    sent = pair.astype(bf)
    lost = lax.dynamic_index_in_dim(pair, lax.axis_index(LINE), 0, keepdims=False)
    lost = lost - lost.astype(bf).astype(f4)
    sent, lost = lax.optimization_barrier((sent, lost))
    summed = jnp.sum(swap(sent, LINE).astype(f4), axis=0) + lost
    value, slope = gelu_pair(summed[0])
    acts = jnp.stack([value, summed[1] * slope]).astype(bf)
    acts = spread(acts, LINE, 4).reshape(1, 8 * quarter, units)
    acts = lax.all_gather(acts, "core", axis=0, tiled=True).reshape(8, 2, quarter, units)

    terms = pl.pallas_call(
        second_kernel,
        in_specs=[smem, vmem, vmem, vmem],
        out_specs=vmem,
        out_shape=jax.ShapeDtypeStruct((NEARS, FARS * rows, 2 * width), bf),
        scratch_shapes=scratch,
        compiler_params=params,
        cost_estimate=cost,
        name="output_terms",
    )(mask, acts, up_weight, down_weight)

    terms = near_swap(terms)
    terms, acts, near = lax.optimization_barrier((terms, acts, near))
    sums = jnp.sum(terms.astype(f4), axis=0).astype(bf)
    sums = sums.reshape(FARS, rows, 2 * width)
    sums, acts, near = lax.optimization_barrier((sums, acts, near))
    sums = swap(sums, FAR)
    up_grad, down_grad = pl.pallas_call(
        third_kernel,
        in_specs=[smem, vmem, hbm],
        out_specs=[vmem, vmem],
        out_shape=masked,
        scratch_shapes=[pltpu.VMEM(near.shape, bf), pltpu.SemaphoreType.DMA((NEARS,))],
        compiler_params=pltpu.CompilerParams(vmem_limit_bytes=LARGE_VMEM_BYTES),
        cost_estimate=cost,
        name="weight_grads",
    )(mask, acts, near)
    sums, up_grad, down_grad = lax.optimization_barrier((sums, up_grad, down_grad))
    totals = jnp.sum(sums.astype(f4), axis=0).astype(bf)
    return (totals[:, :width], totals[:, width:], up_grad, down_grad)


def solution(mesh):
    fine = Mesh(mesh.devices.reshape(SIZES), AXES)
    in_specs = (P(ROW, COL), P(COL, ROW), P(ROW, COL), P(ROW, COL), P())
    out_specs = (P(ROW, COL), P(ROW, COL), P(COL, ROW), P(ROW, COL))
    return jax.shard_map(local, mesh=fine, in_specs=in_specs, out_specs=out_specs, check_vma=False)
```

```python
import math

import jax
import jax.numpy as jnp
import numpy as np
from jax import lax
from jax.experimental import pallas as pl
from jax.experimental.pallas import tpu as pltpu
from jax.sharding import Mesh, PartitionSpec as P

BLK = 128
AXES = ("zh", "zl", "xh", "xl", "yh", "ylh", "yll", "core")
SIZES = (4, 2, 2, 2, 2, 2, 2, 2)
ROW = ("zh", "zl", "xh", "xl", "yh")
COL = ("ylh", "yll", "core")
FAR = ("xh", "zh", "yh")
FARS = 16
NEARS = 4
LINE = ("yll", "ylh")
VMEM_BYTES = 12 * 1024 * 1024
LARGE_VMEM_BYTES = 56 * 1024 * 1024

slope_coef = 0.7978845608
cubic_coef = 0.044715


def gelu_pair(values):
    tangent = jnp.tanh(slope_coef * (values + cubic_coef * values * values * values))
    value = 0.5 * values * (1.0 + tangent)
    slope = 0.5 * (1.0 + tangent) + 0.5 * values * (1.0 - tangent * tangent) * slope_coef * (
        1.0 + 3.0 * cubic_coef * values * values
    )
    return value, slope


def near_groups():
    order = np.arange(math.prod(SIZES)).reshape(8, 4, 2, 4, 2)
    groups = []
    for yh, yl, core, zp, xp in np.ndindex(2, 4, 2, 4, 2):
        zs = sorted(((2 * zp + core) % 8, (2 * zp + core + 1) % 8), key=lambda z: z % 2)
        xs = sorted(((2 * xp + core) % 4, (2 * xp + core + 1) % 4), key=lambda x: x % 2)
        groups.append([int(order[z, x, yh, yl, core]) for x in xs for z in zs])
    return groups


def near_swap(blocks):
    return lax.all_to_all(
        blocks, AXES, split_axis=0, concat_axis=0, tiled=True, axis_index_groups=near_groups()
    )


def spread(block, axes, count):
    copies = jnp.broadcast_to(block[None], (count,) + block.shape)
    return lax.all_to_all(copies, axes, split_axis=0, concat_axis=0, tiled=True)


def swap(blocks, axes):
    return lax.all_to_all(blocks, axes, split_axis=0, concat_axis=0, tiled=True)


def kept(mask_ref, d_block, f_block, block):
    return jnp.where(mask_ref[d_block, f_block] != 0, block, jnp.zeros_like(block))


def dot(a, b, axis_a, axis_b):
    dims = (((axis_a,), (axis_b,)), ((), ()))
    return lax.dot_general(a, b, dims, preferred_element_type=jnp.float32)


def mask_weights(mask_ref, up_ref, down_ref, um, dm):
    width, units = um.shape
    for i in range(width // BLK):
        d = slice(i * BLK, (i + 1) * BLK)
        for j in range(units // BLK):
            f = slice(j * BLK, (j + 1) * BLK)
            um[d, f] = kept(mask_ref, i, j, up_ref[d, f])
            dm[f, d] = kept(mask_ref, i, j, down_ref[f, d])


def first_kernel(
    core_ref, mask_ref, near_ref, up_ref, down_ref, keep_ref, give_ref, um, dm
):
    mask_weights(mask_ref, up_ref, down_ref, um, dm)
    width = um.shape[0]
    half = keep_ref.shape[1]
    hidden = dot(near_ref[:, :, :width].reshape(2 * half, width), um[...], 1, 0)
    grad = dot(near_ref[:, :, width:].reshape(2 * half, width), dm[...], 1, 1)
    low = core_ref[0] == 0
    for k, part in enumerate((hidden, grad)):
        a, b = part[:half], part[half:]
        keep_ref[k] = jnp.where(low, a, b)
        give_ref[k] = jnp.where(low, b, a)


def second_kernel(mask_ref, acts_ref, up_ref, down_ref, terms_ref, um, dm):
    mask_weights(mask_ref, up_ref, down_ref, um, dm)
    blocks, _, rows, units = acts_ref.shape
    width = um.shape[0]
    wide = width // 3
    act = acts_ref[:, 0].reshape(blocks * rows, units)
    dact = acts_ref[:, 1].reshape(blocks * rows, units)
    blocks, rows, _ = terms_ref.shape
    for k in range(3):
        w = slice(k * wide, (k + 1) * wide)
        out = dot(act, dm[:, w], 1, 0).astype(terms_ref.dtype)
        terms_ref[:, :, w] = out.reshape(blocks, rows, wide)
        back = dot(dact, um[w, :], 1, 1).astype(terms_ref.dtype)
        terms_ref[:, :, width + k * wide : width + (k + 1) * wide] = back.reshape(blocks, rows, wide)


def third_kernel(mask_ref, acts_ref, saved_ref, upg_ref, downg_ref, near_ref, sem):
    loading = [
        pltpu.make_async_copy(saved_ref.at[i], near_ref.at[i], sem.at[i])
        for i in range(near_ref.shape[0])
    ]
    for copy in loading:
        copy.start()
    for copy in loading:
        copy.wait()
    blocks, _, rows, units = acts_ref.shape
    width = upg_ref.shape[0]
    wide = width // 3
    tokens = blocks * rows
    act = acts_ref[:, 0].reshape(tokens, units)
    dact = acts_ref[:, 1].reshape(tokens, units)
    for k in range(3):
        w = slice(k * wide, (k + 1) * wide)
        g = near_ref[:, :, width + k * wide : width + (k + 1) * wide].reshape(tokens, wide)
        down = dot(act, g, 0, 0).astype(downg_ref.dtype)
        up = dot(near_ref[:, :, w].reshape(tokens, wide), dact, 0, 0).astype(upg_ref.dtype)
        for i in range(wide // BLK):
            d = slice(i * BLK, (i + 1) * BLK)
            at = slice(k * wide + i * BLK, k * wide + (i + 1) * BLK)
            for j in range(units // BLK):
                f = slice(j * BLK, (j + 1) * BLK)
                d_block = k * (wide // BLK) + i
                upg_ref[at, f] = kept(mask_ref, d_block, j, up[d, f])
                downg_ref[f, at] = kept(mask_ref, d_block, j, down[f, d])


def local(inputs, up_weight, down_weight, out_grad, block_mask):
    row_index = lax.axis_index(ROW)
    col_index = lax.axis_index(COL)
    core = lax.axis_index("core")
    rows, width = inputs.shape
    units = up_weight.shape[1]
    d_blocks = width // BLK
    f_blocks = units // BLK
    tokens = 64 * rows
    half = tokens // 2
    quarter = half // 4
    bf, f4 = jnp.bfloat16, jnp.float32
    smem = pl.BlockSpec(memory_space=pltpu.SMEM)
    vmem = pl.BlockSpec(memory_space=pltpu.VMEM)
    hbm = pl.BlockSpec(memory_space=pltpu.HBM)
    params = pltpu.CompilerParams(vmem_limit_bytes=VMEM_BYTES)
    cost = pl.CostEstimate(
        flops=4 * tokens * width * units,
        bytes_accessed=4 * width * (units + tokens),
        transcendentals=0,
    )
    scratch = [pltpu.VMEM((width, units), bf), pltpu.VMEM((units, width), bf)]
    masked = [jax.ShapeDtypeStruct((width, units), bf), jax.ShapeDtypeStruct((units, width), bf)]

    both = jnp.concatenate([inputs, out_grad], axis=1)
    far = spread(both, FAR, FARS)
    mask = lax.dynamic_slice(
        block_mask, (col_index * d_blocks, row_index * f_blocks), (d_blocks, f_blocks)
    )
    far, mask = lax.optimization_barrier((far, mask))
    far = far.reshape(1, FARS * rows, 2 * width)
    near = near_swap(jnp.broadcast_to(far, (NEARS,) + far.shape[1:]))

    keep, give = pl.pallas_call(
        first_kernel,
        in_specs=[smem, smem, vmem, vmem, vmem],
        out_specs=[vmem, vmem],
        out_shape=[jax.ShapeDtypeStruct((2, half, units), f4)] * 2,
        scratch_shapes=scratch,
        compiler_params=params,
        cost_estimate=cost,
        name="partial_sums",
    )(core.reshape(1), mask, near, up_weight, down_weight)
    pair = keep + lax.ppermute(give, "core", [(0, 1), (1, 0)])
    pair = pair.reshape(2, 4, quarter, units).transpose(1, 0, 2, 3)
    summed = jnp.sum(swap(pair, LINE), axis=0)
    value, slope = gelu_pair(summed[0])
    acts = jnp.stack([value, summed[1] * slope]).astype(bf)
    acts = spread(acts, LINE, 4).reshape(1, 8 * quarter, units)
    acts = lax.all_gather(acts, "core", axis=0, tiled=True).reshape(8, 2, quarter, units)

    terms = pl.pallas_call(
        second_kernel,
        in_specs=[smem, vmem, vmem, vmem],
        out_specs=vmem,
        out_shape=jax.ShapeDtypeStruct((NEARS, FARS * rows, 2 * width), bf),
        scratch_shapes=scratch,
        compiler_params=params,
        cost_estimate=cost,
        name="output_terms",
    )(mask, acts, up_weight, down_weight)

    terms = near_swap(terms)
    terms, acts, near = lax.optimization_barrier((terms, acts, near))
    sums = jnp.sum(terms.astype(f4), axis=0).astype(bf)
    sums = sums.reshape(FARS, rows, 2 * width)
    sums, acts, near = lax.optimization_barrier((sums, acts, near))
    sums = swap(sums, FAR)
    up_grad, down_grad = pl.pallas_call(
        third_kernel,
        in_specs=[smem, vmem, hbm],
        out_specs=[vmem, vmem],
        out_shape=masked,
        scratch_shapes=[pltpu.VMEM(near.shape, bf), pltpu.SemaphoreType.DMA((NEARS,))],
        compiler_params=pltpu.CompilerParams(vmem_limit_bytes=LARGE_VMEM_BYTES),
        cost_estimate=cost,
        name="weight_grads",
    )(mask, acts, near)
    sums, up_grad, down_grad = lax.optimization_barrier((sums, up_grad, down_grad))
    totals = jnp.sum(sums.astype(f4), axis=0).astype(bf)
    return (totals[:, :width], totals[:, width:], up_grad, down_grad)


def solution(mesh):
    fine = Mesh(mesh.devices.reshape(SIZES), AXES)
    in_specs = (P(ROW, COL), P(COL, ROW), P(ROW, COL), P(ROW, COL), P())
    out_specs = (P(ROW, COL), P(ROW, COL), P(COL, ROW), P(ROW, COL))
    return jax.shard_map(local, mesh=fine, in_specs=in_specs, out_specs=out_specs, check_vma=False)
```

```python
import math

import jax
import jax.numpy as jnp
import numpy as np
from jax import lax
from jax.experimental import pallas as pl
from jax.experimental.pallas import tpu as pltpu
from jax.sharding import Mesh, PartitionSpec as P

BLK = 128
AXES = ("zh", "zl", "xh", "xl", "yh", "ylh", "yll", "core")
SIZES = (4, 2, 2, 2, 2, 2, 2, 2)
ROW = ("zh", "zl", "xh", "xl", "yh")
COL = ("ylh", "yll", "core")
FAR = ("xh", "zh", "yh")
FARS = 16
NEARS = 4
LINE = ("yll", "ylh")
VMEM_BYTES = 12 * 1024 * 1024
LARGE_VMEM_BYTES = 56 * 1024 * 1024

slope_coef = 0.7978845608
cubic_coef = 0.044715


def gelu_pair(values):
    tangent = jnp.tanh(slope_coef * (values + cubic_coef * values * values * values))
    value = 0.5 * values * (1.0 + tangent)
    slope = 0.5 * (1.0 + tangent) + 0.5 * values * (1.0 - tangent * tangent) * slope_coef * (
        1.0 + 3.0 * cubic_coef * values * values
    )
    return value, slope


def near_groups():
    order = np.arange(math.prod(SIZES)).reshape(8, 4, 2, 4, 2)
    groups = []
    for yh, yl, core, zp, xp in np.ndindex(2, 4, 2, 4, 2):
        zs = sorted(((2 * zp + core) % 8, (2 * zp + core + 1) % 8), key=lambda z: z % 2)
        xs = sorted(((2 * xp + core) % 4, (2 * xp + core + 1) % 4), key=lambda x: x % 2)
        groups.append([int(order[z, x, yh, yl, core]) for x in xs for z in zs])
    return groups


def near_swap(blocks):
    return lax.all_to_all(
        blocks, AXES, split_axis=0, concat_axis=0, tiled=True, axis_index_groups=near_groups()
    )


def spread(block, axes, count):
    copies = jnp.broadcast_to(block[None], (count,) + block.shape)
    return lax.all_to_all(copies, axes, split_axis=0, concat_axis=0, tiled=True)


def swap(blocks, axes):
    return lax.all_to_all(blocks, axes, split_axis=0, concat_axis=0, tiled=True)


def kept(mask_ref, d_block, f_block, block):
    return jnp.where(mask_ref[d_block, f_block] != 0, block, jnp.zeros_like(block))


def dot(a, b, axis_a, axis_b):
    dims = (((axis_a,), (axis_b,)), ((), ()))
    return lax.dot_general(a, b, dims, preferred_element_type=jnp.float32)


def mask_weights(mask_ref, up_ref, down_ref, um, dm):
    width, units = um.shape
    for i in range(width // BLK):
        d = slice(i * BLK, (i + 1) * BLK)
        for j in range(units // BLK):
            f = slice(j * BLK, (j + 1) * BLK)
            um[d, f] = kept(mask_ref, i, j, up_ref[d, f])
            dm[f, d] = kept(mask_ref, i, j, down_ref[f, d])


def first_kernel(half_ref, mask_ref, near_ref, up_ref, down_ref, part_ref, um, dm):
    mask_weights(mask_ref, up_ref, down_ref, um, dm)
    width = um.shape[0]
    half = part_ref.shape[1]
    blocks = near_ref.shape[0] // 2
    at = pl.ds(half_ref[0] * blocks, blocks)
    part_ref[0] = dot(near_ref[at, :, :width].reshape(half, width), um[...], 1, 0)
    part_ref[1] = dot(near_ref[at, :, width:].reshape(half, width), dm[...], 1, 1)


def second_kernel(mask_ref, acts_ref, up_ref, down_ref, terms_ref, um, dm):
    mask_weights(mask_ref, up_ref, down_ref, um, dm)
    blocks, _, rows, units = acts_ref.shape
    width = um.shape[0]
    wide = width // 3
    act = acts_ref[:, 0].reshape(blocks * rows, units)
    dact = acts_ref[:, 1].reshape(blocks * rows, units)
    blocks, rows, _ = terms_ref.shape
    for k in range(3):
        w = slice(k * wide, (k + 1) * wide)
        out = dot(act, dm[:, w], 1, 0).astype(terms_ref.dtype)
        terms_ref[:, :, w] = out.reshape(blocks, rows, wide)
        back = dot(dact, um[w, :], 1, 1).astype(terms_ref.dtype)
        terms_ref[:, :, width + k * wide : width + (k + 1) * wide] = back.reshape(blocks, rows, wide)


def third_kernel(mask_ref, acts_ref, saved_ref, upg_ref, downg_ref, near_ref, sem):
    loading = [
        pltpu.make_async_copy(saved_ref.at[i], near_ref.at[i], sem.at[i])
        for i in range(near_ref.shape[0])
    ]
    for copy in loading:
        copy.start()
    for copy in loading:
        copy.wait()
    blocks, _, rows, units = acts_ref.shape
    width = upg_ref.shape[0]
    wide = width // 3
    tokens = blocks * rows
    act = acts_ref[:, 0].reshape(tokens, units)
    dact = acts_ref[:, 1].reshape(tokens, units)
    for k in range(3):
        w = slice(k * wide, (k + 1) * wide)
        g = near_ref[:, :, width + k * wide : width + (k + 1) * wide].reshape(tokens, wide)
        down = dot(act, g, 0, 0).astype(downg_ref.dtype)
        up = dot(near_ref[:, :, w].reshape(tokens, wide), dact, 0, 0).astype(upg_ref.dtype)
        for i in range(wide // BLK):
            d = slice(i * BLK, (i + 1) * BLK)
            at = slice(k * wide + i * BLK, k * wide + (i + 1) * BLK)
            for j in range(units // BLK):
                f = slice(j * BLK, (j + 1) * BLK)
                d_block = k * (wide // BLK) + i
                upg_ref[at, f] = kept(mask_ref, d_block, j, up[d, f])
                downg_ref[f, at] = kept(mask_ref, d_block, j, down[f, d])


def local(inputs, up_weight, down_weight, out_grad, block_mask):
    row_index = lax.axis_index(ROW)
    col_index = lax.axis_index(COL)
    core = lax.axis_index("core")
    rows, width = inputs.shape
    units = up_weight.shape[1]
    d_blocks = width // BLK
    f_blocks = units // BLK
    tokens = 64 * rows
    half = tokens // 2
    quarter = half // 4
    bf, f4 = jnp.bfloat16, jnp.float32
    smem = pl.BlockSpec(memory_space=pltpu.SMEM)
    vmem = pl.BlockSpec(memory_space=pltpu.VMEM)
    hbm = pl.BlockSpec(memory_space=pltpu.HBM)
    params = pltpu.CompilerParams(vmem_limit_bytes=VMEM_BYTES)
    cost = pl.CostEstimate(
        flops=4 * tokens * width * units,
        bytes_accessed=4 * width * (units + tokens),
        transcendentals=0,
    )
    scratch = [pltpu.VMEM((width, units), bf), pltpu.VMEM((units, width), bf)]
    masked = [jax.ShapeDtypeStruct((width, units), bf), jax.ShapeDtypeStruct((units, width), bf)]

    both = jnp.concatenate([inputs, out_grad], axis=1)
    far = spread(both, FAR, FARS)
    mask = lax.dynamic_slice(
        block_mask, (col_index * d_blocks, row_index * f_blocks), (d_blocks, f_blocks)
    )
    far, mask = lax.optimization_barrier((far, mask))
    far = far.reshape(1, FARS * rows, 2 * width)
    near = near_swap(jnp.broadcast_to(far, (NEARS,) + far.shape[1:]))

    partial_sums = pl.pallas_call(
        first_kernel,
        in_specs=[smem, smem, vmem, vmem, vmem],
        out_specs=vmem,
        out_shape=jax.ShapeDtypeStruct((2, half, units), f4),
        scratch_shapes=scratch,
        compiler_params=params,
        cost_estimate=cost,
        name="partial_sums",
    )
    give = partial_sums((1 - core).reshape(1), mask, near, up_weight, down_weight)
    got = lax.ppermute(give, "core", [(0, 1), (1, 0)])
    keep = partial_sums(core.reshape(1), mask, near, up_weight, down_weight)
    pair = keep + got
    pair = pair.reshape(2, 4, quarter, units).transpose(1, 0, 2, 3)
    sent = pair.astype(bf)
    lost = lax.dynamic_index_in_dim(pair, lax.axis_index(LINE), 0, keepdims=False)
    lost = lost - lost.astype(bf).astype(f4)
    sent, lost = lax.optimization_barrier((sent, lost))
    summed = jnp.sum(swap(sent, LINE).astype(f4), axis=0) + lost
    value, slope = gelu_pair(summed[0])
    acts = jnp.stack([value, summed[1] * slope]).astype(bf)
    acts = spread(acts, LINE, 4).reshape(1, 8 * quarter, units)
    acts = lax.all_gather(acts, "core", axis=0, tiled=True).reshape(8, 2, quarter, units)

    terms = pl.pallas_call(
        second_kernel,
        in_specs=[smem, vmem, vmem, vmem],
        out_specs=vmem,
        out_shape=jax.ShapeDtypeStruct((NEARS, FARS * rows, 2 * width), bf),
        scratch_shapes=scratch,
        compiler_params=params,
        cost_estimate=cost,
        name="output_terms",
    )(mask, acts, up_weight, down_weight)

    terms = near_swap(terms)
    terms, acts, near = lax.optimization_barrier((terms, acts, near))
    sums = jnp.sum(terms.astype(f4), axis=0).astype(bf)
    sums = sums.reshape(FARS, rows, 2 * width)
    sums, acts, near = lax.optimization_barrier((sums, acts, near))
    sums = swap(sums, FAR)
    up_grad, down_grad = pl.pallas_call(
        third_kernel,
        in_specs=[smem, vmem, hbm],
        out_specs=[vmem, vmem],
        out_shape=masked,
        scratch_shapes=[pltpu.VMEM(near.shape, bf), pltpu.SemaphoreType.DMA((NEARS,))],
        compiler_params=pltpu.CompilerParams(vmem_limit_bytes=LARGE_VMEM_BYTES),
        cost_estimate=cost,
        name="weight_grads",
    )(mask, acts, near)
    sums, up_grad, down_grad = lax.optimization_barrier((sums, up_grad, down_grad))
    totals = jnp.sum(sums.astype(f4), axis=0).astype(bf)
    return (totals[:, :width], totals[:, width:], up_grad, down_grad)


def solution(mesh):
    fine = Mesh(mesh.devices.reshape(SIZES), AXES)
    in_specs = (P(ROW, COL), P(COL, ROW), P(ROW, COL), P(ROW, COL), P())
    out_specs = (P(ROW, COL), P(ROW, COL), P(COL, ROW), P(ROW, COL))
    return jax.shard_map(local, mesh=fine, in_specs=in_specs, out_specs=out_specs, check_vma=False)
```
